32 devices in a mesh: mol: 8 (over y, x, core), frag: 4 (over z).
Axes of the slice: x: 2, y: 2, z: 4, core: 2. Of those that a mesh axis runs over, the one named last changes fastest.
Arguments:
- counts: bfloat16 [16384, 16384], P('mol', 'frag'), may hold values from 0 to 16, as said below
- mol_factor: bfloat16 [16384, 256], P('mol', 'frag'), may hold values from 0.0049 to 2, as said below
- frag_factor: bfloat16 [256, 16384], P('mol', 'frag'), may hold values from 0.0014 to 0.61, as said below
Outputs:
- new_mol: bfloat16 [16384, 256], P('mol', 'frag')
- new_frag: bfloat16 [256, 16384], P('mol', 'frag')
The draws below stay inside these ranges and needn't reach their ends.
Inputs may be any that keep to these rules, and one draw needn't show every extreme that they name: `counts`: whole numbers, held exactly. `mol_factor`: positive entries. `frag_factor`: positive entries.
All inputs are finite; a program needn't handle non-finite values.
Results may differ from the reference program's by a relative error of at most 0.0034.
Values may be sent and summed in bfloat16 or wider, within the bound.
A program may use at most 128 MiB of HBM per device.

```python
import jax
import jax.numpy as jnp

FRAGS = 16384
RANK = 256
MOLS = 16384


def cluster_layout(key):
    member = jax.random.randint(jax.random.fold_in(key, 101), (MOLS,), 0, RANK)
    group = jax.random.permutation(jax.random.fold_in(key, 102), FRAGS) % RANK
    strong = jax.random.randint(jax.random.fold_in(key, 103), (RANK, RANK), 0, 4) == 0
    return (member, group, strong)


def log_uniform(key, shape, lowest, highest):
    return jnp.exp(jax.random.uniform(key, shape, jnp.float32, jnp.log(lowest), jnp.log(highest)))


def draw_counts(key, part):
    member, group, strong = cluster_layout(key)
    key = jax.random.fold_in(key, 11)
    ceiling = jnp.where(strong[member][:, group], 16, 2)
    values = jax.random.randint(key, (MOLS, FRAGS), 0, ceiling + 1)
    return values.astype(jnp.float32).astype(jnp.bfloat16)


def draw_mol_factor(key, part):
    member, group, strong = cluster_layout(key)
    key = jax.random.fold_in(key, 12)
    level_key, noise_key = jax.random.split(key)
    level = log_uniform(level_key, (RANK, RANK), 0.01, 1.0)
    noise = log_uniform(noise_key, (MOLS, RANK), 0.5, 2.0)
    return (level[member] * noise).astype(jnp.bfloat16)


def draw_frag_factor(key, part):
    member, group, strong = cluster_layout(key)
    key = jax.random.fold_in(key, 13)
    level_key, noise_key = jax.random.split(key)
    level = log_uniform(level_key, (RANK, RANK), 0.003, 0.3)
    noise = log_uniform(noise_key, (RANK, FRAGS), 0.5, 2.0)
    return (level[:, group] * noise).astype(jnp.bfloat16)


def setup_inputs(seed: int = 0) -> dict:
    key_of = jax.random.split(jax.random.key(seed), 4)
    counts = draw_counts(jax.random.fold_in(key_of[3], 71), 0)
    mol_factor = draw_mol_factor(jax.random.fold_in(key_of[3], 71), 0)
    frag_factor = draw_frag_factor(jax.random.fold_in(key_of[3], 71), 0)
    return dict(counts=counts, mol_factor=mol_factor, frag_factor=frag_factor)


def reference(counts, mol_factor, frag_factor):
    numer_mol = jnp.dot(counts, frag_factor.T, preferred_element_type=jnp.float32)
    gram_frag = jnp.dot(frag_factor, frag_factor.T, preferred_element_type=jnp.float32).astype(jnp.bfloat16)
    denom_mol = jnp.dot(mol_factor, gram_frag, preferred_element_type=jnp.float32)
    new_mol = (mol_factor.astype(jnp.float32) * numer_mol / denom_mol).astype(jnp.bfloat16)
    numer_frag = jnp.dot(new_mol.T, counts, preferred_element_type=jnp.float32)
    gram_mol = jnp.dot(new_mol.T, new_mol, preferred_element_type=jnp.float32).astype(jnp.bfloat16)
    denom_frag = jnp.dot(gram_mol, frag_factor, preferred_element_type=jnp.float32)
    new_frag = (frag_factor.astype(jnp.float32) * numer_frag / denom_frag).astype(jnp.bfloat16)
    return new_mol, new_frag
```

```python
import functools

import jax
import jax.numpy as jnp
from jax import lax
from jax.experimental import pallas as pl
from jax.experimental.pallas import tpu as pltpu
from jax.sharding import PartitionSpec as P

CONTRACT_LAST = (((1,), (1,)), ((), ()))
CONTRACT_FIRST = (((0,), (0,)), ((), ()))


def product(left, right, dims):
    return lax.dot_general(left, right, dims, preferred_element_type=jnp.float32)


def body(counts, mol_factor, frag_factor):
    rank_cols = mol_factor.shape[1]
    rank_rows = frag_factor.shape[0]
    frag_index = lax.axis_index("frag")
    mol_index = lax.axis_index("mol")
    columns = lax.all_gather(frag_factor, "mol", axis=0, tiled=True)
    numer_whole = product(columns, counts, CONTRACT_LAST)
    gram_whole = product(columns, columns, CONTRACT_LAST)
    numer_whole, gram_whole = lax.psum((numer_whole, gram_whole), "frag")
    numer_mine = lax.dynamic_slice_in_dim(numer_whole, frag_index * rank_cols, rank_cols, 0)
    gram_mine = lax.dynamic_slice_in_dim(gram_whole, frag_index * rank_cols, rank_cols, 0)
    gram_mine = gram_mine.astype(jnp.bfloat16)
    denom_mol = product(
        lax.all_gather(mol_factor, "frag", axis=1, tiled=True), gram_mine, CONTRACT_LAST
    )
    new_mol = (mol_factor.astype(jnp.float32) * numer_mine.T / denom_mol).astype(jnp.bfloat16)
    gathered_mol = lax.all_gather(new_mol, "frag", axis=1, tiled=True)
    numer_frag = product(gathered_mol, counts, CONTRACT_FIRST)
    gram_mol = product(gathered_mol, gathered_mol, CONTRACT_FIRST)
    numer_frag, gram_mol = lax.psum((numer_frag, gram_mol), "mol")
    numer_rows = lax.dynamic_slice_in_dim(numer_frag, mol_index * rank_rows, rank_rows, 0)
    gram_rows = lax.dynamic_slice_in_dim(gram_mol, mol_index * rank_rows, rank_rows, 0)
    denom_frag = jnp.dot(
        gram_rows.astype(jnp.bfloat16), columns, preferred_element_type=jnp.float32
    )
    new_frag = (frag_factor.astype(jnp.float32) * numer_rows / denom_frag).astype(jnp.bfloat16)
    return (new_mol, new_frag)


MESH = pl.DeviceIdType.MESH
F32 = jnp.float32
BF16 = jnp.bfloat16
STEPS = 4
TILE = 1024
PARTS = 2


def remote(src, dst, send, recv, mol, frag):
    return pltpu.make_async_remote_copy(
        src_ref=src, dst_ref=dst, send_sem=send, recv_sem=recv,
        device_id={"mol": mol, "frag": frag}, device_id_type=MESH,
    )


def aligned(index, size):
    return pl.ds(pl.multiple_of(index * size, size), size)


def kernel(
    n_mol, n_frag, counts_hbm, w_ref, h_ref, wout, hout,
    counts, hfull, wt, wmine, gpart, gown, gfull, acc,
    up_out, up_in, down_out, down_in, newall, newt, psum, pin, csum, cin,
    counts_sem, h_s, h_r, hc_s, hc_r, w_s, w_r, g_s, g_r, gp_s, gp_r,
    up_s, up_r, down_s, down_r, ag_s, ag_r, c1_s, c1_r, c2_s, c2_r,
):
    chips = n_mol // 2
    last = n_frag - 1
    mols, cols = w_ref.shape
    rows, frags = h_ref.shape
    half = mols // 2
    sub = half // STEPS
    rank = rows * n_mol
    m = lax.axis_index("mol")
    z = lax.axis_index("frag")
    chip = m // 2
    core = m % 2
    twin = chip * 2 + 1 - core
    tiles = frags // TILE
    width = frags // PARTS

    load = pltpu.make_async_copy(counts_hbm, counts, counts_sem)
    load.start()
    hfull[aligned(m, rows), :] = h_ref[...]
    wt[...] = w_ref[...].T

    @pl.when(z == last)
    def _():
        wmine[aligned(z, cols), :] = wt[:, :half]

    @pl.when(z == 0)
    def _():
        wmine[aligned(z, cols), :] = wt[:, half:]

    barrier = pltpu.get_barrier_semaphore()
    for k in range(1, n_mol):
        pl.semaphore_signal(
            barrier, inc=1, device_id={"mol": (m + k) % n_mol, "frag": z}, device_id_type=MESH)
    for k in range(1, n_frag):
        pl.semaphore_signal(
            barrier, inc=1, device_id={"mol": m, "frag": (z + k) % n_frag}, device_id_type=MESH)
    pl.semaphore_wait(barrier, n_mol - 1 + n_frag - 1)

    def h_copy(k, p):
        lanes = pl.ds(p * width, width)
        return remote(
            h_ref.at[:, lanes], hfull.at[aligned(m, rows), lanes],
            h_s.at[k - 1, p], h_r.at[k - 1, p], ((chip + k) % chips) * 2 + core, z)

    def h_twin(k, p):
        lanes = pl.ds(p * width, width)
        there = ((chip + chips - k) % chips) * 2 + core
        block = hfull.at[aligned(there, rows), lanes]
        return remote(
            h_ref.at[:, lanes] if k == 0 else block, block,
            hc_s.at[k, p], hc_r.at[k, p], twin, z)

    for p in range(PARTS):
        for k in range(1, chips):
            h_copy(k, p).start()
        h_twin(0, p).start()

    to_last = remote(wt.at[:, :half], wmine.at[aligned(z, cols), :], w_s.at[0], w_r.at[z], m, last)
    to_first = remote(wt.at[:, half:], wmine.at[aligned(z, cols), :], w_s.at[1], w_r.at[z], m, 0)

    @pl.when(z < last)
    def _():
        to_last.start()

    @pl.when(z > 0)
    def _():
        to_first.start()

    for p in range(PARTS):
        for k in range(1, chips):
            h_copy(k, p).wait_recv()
            h_twin(k, p).start()
    for p in range(PARTS):
        for k in range(chips):
            h_twin(k, p).wait_recv()

    gown[...] = product(h_ref[...], hfull[...], CONTRACT_LAST)
    g_last = remote(gown, gpart.at[z], g_s.at[0], g_r.at[z], m, last)
    g_first = remote(gown, gpart.at[z], g_s.at[1], g_r.at[z], m, 0)

    @pl.when(z < last)
    def _():
        g_last.start()

    @pl.when(z > 0)
    def _():
        g_first.start()

    load.wait()

    def g_share(k):
        block = gfull.at[aligned(m, rows), :]
        return remote(block, block, gp_s.at[k - 1], gp_r.at[k - 1], (m + k) % n_mol, z)

    def owner_ready():
        total = gown[...]
        for k in range(1, n_frag):
            there = (z + k) % n_frag
            remote(gown, gpart.at[there], g_s.at[0], g_r.at[there], m, z).wait_recv()
            total = total + gpart[there]
        gfull[aligned(m, rows), :] = total.astype(BF16)
        for k in range(1, n_mol):
            g_share(k).start()
        for k in range(1, n_frag):
            there = (z + k) % n_frag
            remote(wt.at[:, :half], wmine.at[aligned(there, cols), :], w_s.at[0], w_r.at[there], m, z).wait_recv()
        for k in range(1, n_mol):
            g_share(k).wait_recv()

    def ag_copy(side, s):
        block = newall.at[aligned(s + side * STEPS, sub), :]
        return remote(
            block, block, ag_s.at[side, s], ag_r.at[side, s], m, z - 1 if side == 0 else z + 1)

    def arrived(side, s):
        here = aligned(s + side * STEPS, sub)
        newt[:, here] = newall[here, :].T

    def reduce_step(side, s, outs, ins, send, recv):
        here = aligned(s + side * STEPS, sub)
        acc[...] = product(counts[here, :], hfull[...], CONTRACT_LAST)
        first, end = (0, last) if side == 0 else (last, 0)
        onward = remote(outs.at[s], ins.at[s], send.at[s], recv.at[s], m, z + 1 if side == 0 else z - 1)

        @pl.when(z != first)
        def _():
            onward.wait_recv()
            acc[...] += ins[s].astype(F32)

        @pl.when(z != end)
        def _():
            outs[s] = acc[...].astype(BF16)
            onward.start()

        @pl.when(z == end)
        def _():
            w = wmine[:, aligned(s, sub)].T
            denom = product(w, gfull[...], (((1,), (0,)), ((), ())))
            newall[here, :] = (w.astype(F32) * acc[...] / denom).astype(BF16)
            ag_copy(side, s).start()
            arrived(side, s)

    def gather_step(side, s):
        ag_copy(side, s).wait_recv()

        @pl.when(z != (0 if side == 0 else last))
        def _():
            ag_copy(side, s).start()

        arrived(side, s)

    def within(s):
        return jnp.logical_and(s >= 0, s < STEPS)

    def tick(t, carry):
        @pl.when(jnp.logical_and(t == last, jnp.logical_or(z == 0, z == last)))
        def _():
            owner_ready()

        up = t - z
        down = t - (last - z)
        from_last = t - last - (last - z)
        from_first = t - last - z

        @pl.when(within(up))
        def _():
            reduce_step(0, up, up_out, up_in, up_s, up_r)

        @pl.when(within(down))
        def _():
            reduce_step(1, down, down_out, down_in, down_s, down_r)

        @pl.when(jnp.logical_and(within(from_last), z < last))
        def _():
            gather_step(0, from_last)

        @pl.when(jnp.logical_and(within(from_first), z > 0))
        def _():
            gather_step(1, from_first)

        return carry

    lax.fori_loop(0, STEPS + 2 * last, tick, 0)

    def twin_copy(q, lanes):
        return remote(
            psum.at[:, 1 - core, :, lanes], pin.at[:, :, lanes], c1_s.at[q], c1_r.at[q], twin, z)

    def chip_copy(k, q, lanes):
        there = (chip + k) % chips
        return remote(
            csum.at[there, :, lanes], cin.at[k - 1, :, lanes],
            c2_s.at[k - 1, q], c2_r.at[k - 1, q], there * 2 + core, z)

    def send_twin(q, lanes, part):
        psum[:, :, :, lanes] = part.astype(BF16).reshape(chips, 2, rows, part.shape[1])
        twin_copy(q, lanes).start()

    def send_chips(q, lanes):
        twin_copy(q, lanes).wait_recv()
        both = psum[:, core, :, lanes].astype(F32) + pin[:, :, lanes].astype(F32)
        csum[:, :, lanes] = both.astype(BF16)
        for k in range(1, chips):
            chip_copy(k, q, lanes).start()

    def total(q, lanes):
        for k in range(1, chips):
            chip_copy(k, q, lanes).wait_recv()
        value = psum[chip, core, :, lanes].astype(F32) + pin[chip, :, lanes].astype(F32)
        for k in range(1, chips):
            value = value + cin[k - 1, :, lanes].astype(F32)
        return value

    gram_lanes = pl.ds(frags, rank)
    plain = (((1,), (0,)), ((), ()))
    send_twin(tiles, gram_lanes, product(newt[...], newall[...], plain))

    def second(q, carry):
        lanes = aligned(q, TILE)
        send_twin(q, lanes, product(newt[...], counts[:, lanes], plain))

        @pl.when(q == 0)
        def _():
            send_chips(tiles, gram_lanes)

        @pl.when(q > 0)
        def _():
            send_chips(q - 1, aligned(q - 1, TILE))

        return carry

    lax.fori_loop(0, tiles, second, 0)
    send_chips(tiles - 1, pl.ds((tiles - 1) * TILE, TILE))

    for k in range(n_frag):
        @pl.when(z == k)
        def _(k=k):
            wout[...] = newall[:, k * cols:(k + 1) * cols]

    @pl.when(z < last)
    def _():
        g_last.wait_send()

    @pl.when(z > 0)
    def _():
        g_first.wait_send()

    gram = total(tiles, gram_lanes).astype(BF16)
    gown[...] = gram.astype(F32)

    def finish(q, carry):
        lanes = aligned(q, TILE)
        denom = product(gown[...].astype(BF16), hfull[:, lanes], plain)
        hout[:, lanes] = (h_ref[:, lanes].astype(F32) * total(q, lanes) / denom).astype(BF16)
        return carry

    lax.fori_loop(0, tiles, finish, 0)

    for p in range(PARTS):
        for k in range(1, chips):
            h_copy(k, p).wait_send()
        for k in range(chips):
            h_twin(k, p).wait_send()

    @pl.when(z < last)
    def _():
        to_last.wait_send()

    @pl.when(z > 0)
    def _():
        to_first.wait_send()

    @pl.when(jnp.logical_or(z == 0, z == last))
    def _():
        for k in range(1, n_mol):
            g_share(k).wait_send()

    def drain(s, carry):
        @pl.when(z < last)
        def _():
            remote(up_out.at[s], up_in.at[s], up_s.at[s], up_r.at[s], m, z + 1).wait_send()
            ag_copy(1, s).wait_send()

        @pl.when(z > 0)
        def _():
            remote(down_out.at[s], down_in.at[s], down_s.at[s], down_r.at[s], m, z - 1).wait_send()
            ag_copy(0, s).wait_send()

        return carry

    lax.fori_loop(0, STEPS, drain, 0)

    def drain_tile(q, carry):
        lanes = aligned(q, TILE)
        twin_copy(q, lanes).wait_send()
        for k in range(1, chips):
            chip_copy(k, q, lanes).wait_send()
        return carry

    lax.fori_loop(0, tiles, drain_tile, 0)
    twin_copy(tiles, gram_lanes).wait_send()
    for k in range(1, chips):
        chip_copy(k, tiles, gram_lanes).wait_send()


def fused(n_mol, n_frag, counts, mol_factor, frag_factor):
    mols, cols = mol_factor.shape
    rows, frags = frag_factor.shape
    rank = rows * n_mol
    chips = n_mol // 2
    half = mols // 2
    sub = half // STEPS
    tiles = frags // TILE
    dma = pltpu.SemaphoreType.DMA
    vmem = pltpu.VMEM
    scratch = [
        vmem((mols, frags), BF16),
        vmem((rank, frags), BF16),
        vmem((cols, mols), BF16),
        vmem((rank, half), BF16),
        vmem((n_frag, rows, rank), F32),
        vmem((rows, rank), F32),
        vmem((rank, rank), BF16),
        vmem((sub, rank), F32),
        vmem((STEPS, sub, rank), BF16),
        vmem((STEPS, sub, rank), BF16),
        vmem((STEPS, sub, rank), BF16),
        vmem((STEPS, sub, rank), BF16),
        vmem((mols, rank), BF16),
        vmem((rank, mols), BF16),
        vmem((chips, 2, rows, frags + rank), BF16),
        vmem((chips, rows, frags + rank), BF16),
        vmem((chips, rows, frags + rank), BF16),
        vmem((chips - 1, rows, frags + rank), BF16),
        dma,
        dma((chips - 1, PARTS)), dma((chips - 1, PARTS)),
        dma((chips, PARTS)), dma((chips, PARTS)),
        dma((2,)), dma((n_frag,)),
        dma((2,)), dma((n_frag,)),
        dma((n_mol - 1,)), dma((n_mol - 1,)),
        dma((STEPS,)), dma((STEPS,)), dma((STEPS,)), dma((STEPS,)),
        dma((2, STEPS)), dma((2, STEPS)),
        dma((tiles + 1,)), dma((tiles + 1,)),
        dma((chips - 1, tiles + 1)), dma((chips - 1, tiles + 1)),
    ]
    return pl.pallas_call(
        functools.partial(kernel, n_mol, n_frag),
        out_shape=(
            jax.ShapeDtypeStruct((mols, cols), BF16),
            jax.ShapeDtypeStruct((rows, frags), BF16),
        ),
        in_specs=[
            pl.BlockSpec(memory_space=pl.ANY),
            pl.BlockSpec(memory_space=pltpu.VMEM),
            pl.BlockSpec(memory_space=pltpu.VMEM),
        ],
        out_specs=(
            pl.BlockSpec(memory_space=pltpu.VMEM),
            pl.BlockSpec(memory_space=pltpu.VMEM),
        ),
        scratch_shapes=scratch,
        compiler_params=pltpu.CompilerParams(
            collective_id=0, has_side_effects=True, vmem_limit_bytes=56 * 1024 * 1024
        ),
        cost_estimate=pl.CostEstimate(
            flops=4 * mols * frags * rank, bytes_accessed=2 * mols * frags, transcendentals=0
        ),
    )(counts, mol_factor, frag_factor)


def fits(n_mol, n_frag, mols, cols, rows, frags):
    return (
        n_mol % 2 == 0 and n_mol > 2 and n_frag > 1 and rows % 16 == 0 and cols % 16 == 0
        and mols % (2 * STEPS * 128) == 0 and frags % (TILE * PARTS) == 0
        and (rows * n_mol) % 128 == 0 and mols * frags <= 2 ** 23 and n_mol <= 8
    )


def solution(mesh):
    n_mol, n_frag = mesh.shape["mol"], mesh.shape["frag"]

    def local(counts, mol_factor, frag_factor):
        if fits(n_mol, n_frag, *mol_factor.shape, *frag_factor.shape):
            return fused(n_mol, n_frag, counts, mol_factor, frag_factor)
        return body(counts, mol_factor, frag_factor)

    return jax.shard_map(
        local,
        mesh=mesh,
        in_specs=(P("mol", "frag"), P("mol", "frag"), P("mol", "frag")),
        out_specs=(P("mol", "frag"), P("mol", "frag")),
        check_vma=False,
    )
```

```python
import functools

import jax
import jax.numpy as jnp
from jax import lax
from jax.experimental import pallas as pl
from jax.experimental.pallas import tpu as pltpu
from jax.sharding import PartitionSpec as P

CONTRACT_LAST = (((1,), (1,)), ((), ()))
CONTRACT_FIRST = (((0,), (0,)), ((), ()))


def product(left, right, dims):
    return lax.dot_general(left, right, dims, preferred_element_type=jnp.float32)


def body(counts, mol_factor, frag_factor):
    rank_cols = mol_factor.shape[1]
    rank_rows = frag_factor.shape[0]
    frag_index = lax.axis_index("frag")
    mol_index = lax.axis_index("mol")
    columns = lax.all_gather(frag_factor, "mol", axis=0, tiled=True)
    numer_whole = product(columns, counts, CONTRACT_LAST)
    gram_whole = product(columns, columns, CONTRACT_LAST)
    numer_whole, gram_whole = lax.psum((numer_whole, gram_whole), "frag")
    numer_mine = lax.dynamic_slice_in_dim(numer_whole, frag_index * rank_cols, rank_cols, 0)
    gram_mine = lax.dynamic_slice_in_dim(gram_whole, frag_index * rank_cols, rank_cols, 0)
    gram_mine = gram_mine.astype(jnp.bfloat16)
    denom_mol = product(
        lax.all_gather(mol_factor, "frag", axis=1, tiled=True), gram_mine, CONTRACT_LAST
    )
    new_mol = (mol_factor.astype(jnp.float32) * numer_mine.T / denom_mol).astype(jnp.bfloat16)
    gathered_mol = lax.all_gather(new_mol, "frag", axis=1, tiled=True)
    numer_frag = product(gathered_mol, counts, CONTRACT_FIRST)
    gram_mol = product(gathered_mol, gathered_mol, CONTRACT_FIRST)
    numer_frag, gram_mol = lax.psum((numer_frag, gram_mol), "mol")
    numer_rows = lax.dynamic_slice_in_dim(numer_frag, mol_index * rank_rows, rank_rows, 0)
    gram_rows = lax.dynamic_slice_in_dim(gram_mol, mol_index * rank_rows, rank_rows, 0)
    denom_frag = jnp.dot(
        gram_rows.astype(jnp.bfloat16), columns, preferred_element_type=jnp.float32
    )
    new_frag = (frag_factor.astype(jnp.float32) * numer_rows / denom_frag).astype(jnp.bfloat16)
    return (new_mol, new_frag)


MESH = pl.DeviceIdType.MESH
F32 = jnp.float32
BF16 = jnp.bfloat16
PLAIN = (((1,), (0,)), ((), ()))
STEPS = 16
GROUP = 2
LAG = 2
TILE = 512
PARTS = 2


def remote(src, dst, send, recv, mol, frag):
    return pltpu.make_async_remote_copy(
        src_ref=src, dst_ref=dst, send_sem=send, recv_sem=recv,
        device_id={"mol": mol, "frag": frag}, device_id_type=MESH,
    )


def aligned(index, size):
    return pl.ds(pl.multiple_of(index * size, size), size)


def kernel(
    n_mol, n_frag, counts_hbm, wt, h_ref, wout, hout,
    counts, hfull, wmine, gpart, gown, gfull, mine,
    edge_out, edge_in, mid_out, mid_in, newall, newt, ahead_sum, psum, pin, csum, cin,
    counts_sem, h_s, h_r, hc_s, hc_r, w_s, w_r, g_s, g_r, gp_s, gp_r,
    edge_s, edge_r, mid_s, mid_r, ag_s, ag_r, c1_s, c1_r, c2_s, c2_r,
):
    chips = n_mol // 2
    cols, mols = wt.shape
    rows, frags = h_ref.shape
    half = mols // 2
    sub = mols // STEPS
    rank = rows * n_mol
    block = 2 * frags // STEPS
    m = lax.axis_index("mol")
    z = lax.axis_index("frag")
    chip = m // 2
    core = m % 2
    twin = chip * 2 + 1 - core
    inner = jnp.logical_or(z == 1, z == 2)
    outer = jnp.logical_not(inner)
    pair = z + 1 - 2 * (z % 2)
    across = 3 - z
    tiles = frags // TILE
    width = frags // PARTS

    load = pltpu.make_async_copy(counts_hbm, counts, counts_sem)
    load.start()
    hfull[aligned(m, rows), :] = h_ref[...]

    @pl.when(inner)
    def _():
        wmine[aligned(z, cols), :] = wt[...]

    barrier = pltpu.get_barrier_semaphore()
    for k in range(1, n_mol):
        pl.semaphore_signal(
            barrier, inc=1, device_id={"mol": (m + k) % n_mol, "frag": z}, device_id_type=MESH)
    for k in range(1, n_frag):
        pl.semaphore_signal(
            barrier, inc=1, device_id={"mol": m, "frag": (z + k) % n_frag}, device_id_type=MESH)
    pl.semaphore_wait(barrier, n_mol - 1 + n_frag - 1)

    def h_copy(k, p):
        lanes = pl.ds(p * width, width)
        return remote(
            h_ref.at[:, lanes], hfull.at[aligned(m, rows), lanes],
            h_s.at[k - 1, p], h_r.at[k - 1, p], ((chip + k) % chips) * 2 + core, z)

    def h_twin(k, p):
        lanes = pl.ds(p * width, width)
        there = ((chip + chips - k) % chips) * 2 + core
        block = hfull.at[aligned(there, rows), lanes]
        return remote(
            h_ref.at[:, lanes] if k == 0 else block, block,
            hc_s.at[k, p], hc_r.at[k, p], twin, z)

    for p in range(PARTS):
        for k in range(1, chips):
            h_copy(k, p).start()
        h_twin(0, p).start()

    w_copies = [
        remote(wt, wmine.at[aligned(z, cols), :], w_s.at[e], w_r.at[z], m, e + 1) for e in range(2)
    ]
    for e in range(2):
        @pl.when(z != e + 1)
        def _(e=e):
            w_copies[e].start()

    for p in range(PARTS):
        for k in range(1, chips):
            h_copy(k, p).wait_recv()
            h_twin(k, p).start()
    for p in range(PARTS):
        for k in range(chips):
            h_twin(k, p).wait_recv()

    g_copies = [remote(gown, gpart.at[z], g_s.at[e], g_r.at[z], m, e + 1) for e in range(2)]
    def share_gram():
        gown[...] = product(h_ref[...], hfull[...], CONTRACT_LAST)
        for e in range(2):
            @pl.when(z != e + 1)
            def _(e=e):
                g_copies[e].start()

    load.wait()

    def g_share(k):
        block = gfull.at[aligned(m, rows), :]
        return remote(block, block, gp_s.at[k - 1], gp_r.at[k - 1], (m + k) % n_mol, z)

    def owner_ready():
        total = gown[...]
        for k in range(1, n_frag):
            there = (z + k) % n_frag
            remote(gown, gpart.at[there], g_s.at[0], g_r.at[there], m, z).wait_recv()
            total = total + gpart[there]
        gfull[aligned(m, rows), :] = total.astype(BF16)
        for k in range(1, n_mol):
            g_share(k).start()
        for k in range(1, n_frag):
            there = (z + k) % n_frag
            remote(wt, wmine.at[aligned(there, cols), :], w_s.at[0], w_r.at[there], m, z).wait_recv()
        for k in range(1, n_mol):
            g_share(k).wait_recv()

    def edge_copy(s):
        return remote(edge_out.at[s], edge_in.at[s], edge_s.at[s], edge_r.at[s], m, pair)

    def mid_copy(s):
        return remote(mid_out.at[s], mid_in.at[s], mid_s.at[s], mid_r.at[s], m, across)

    def ag_copy(s):
        part = newall.at[aligned(s, sub), :]
        return remote(part, part, ag_s.at[s], ag_r.at[s], m, pair)

    def arrived(s):
        here = aligned(s, sub)
        newt[:, here] = newall[here, :].T

        @pl.when(s >= STEPS // 2)
        def _():
            lanes = aligned(s - STEPS // 2, block)
            ahead_sum[:, lanes] = product(newt[:, :half], counts[:half, lanes], PLAIN)

    def partial_sum(s):
        @pl.when(s % GROUP == 0)
        def _():
            rows_of = aligned(s // GROUP, GROUP * sub)
            mine[...] = product(counts[rows_of, :], hfull[...], CONTRACT_LAST)

        return mine[aligned(s % GROUP, sub), :]

    @pl.when(outer)
    def _():
        def send(s, carry):
            edge_out[s] = partial_sum(s).astype(BF16)
            edge_copy(s).start()

            @pl.when(s == GROUP - 1)
            def _():
                share_gram()

            return carry

        def take(s, carry):
            ag_copy(s).wait_recv()
            arrived(s)
            return carry

        lax.fori_loop(0, STEPS, send, 0)
        lax.fori_loop(0, STEPS, take, 0)

    @pl.when(inner)
    def _():
        def step(i, carry):
            @pl.when(i < STEPS)
            def _():
                here_sum = partial_sum(i)

                @pl.when(i == 0)
                def _():
                    share_gram()

                edge_copy(i).wait_recv()
                mid_out[i] = (here_sum + edge_in[i].astype(F32)).astype(BF16)
                mid_copy(i).start()

            @pl.when(i == LAG)
            def _():
                owner_ready()

            @pl.when(i >= LAG)
            def _():
                s = i - LAG
                here = aligned(s, sub)
                mid_copy(s).wait_recv()
                numer = mid_out[s].astype(F32) + mid_in[s].astype(F32)
                w = wmine[:, here].T
                denom = product(w, gfull[...], PLAIN)
                newall[here, :] = (w.astype(F32) * numer / denom).astype(BF16)
                ag_copy(s).start()
                arrived(s)

            return carry

        lax.fori_loop(0, STEPS + LAG, step, 0)

    def twin_copy(q, lanes):
        return remote(
            psum.at[:, 1 - core, :, lanes], pin.at[:, :, lanes], c1_s.at[q], c1_r.at[q], twin, z)

    def chip_copy(k, q, lanes):
        there = (chip + k) % chips
        return remote(
            csum.at[there, :, lanes], cin.at[k - 1, :, lanes],
            c2_s.at[k - 1, q], c2_r.at[k - 1, q], there * 2 + core, z)

    def send_twin(q, lanes, part):
        psum[:, :, :, lanes] = part.astype(BF16).reshape(chips, 2, rows, part.shape[1])
        twin_copy(q, lanes).start()

    def send_chips(q, lanes):
        twin_copy(q, lanes).wait_recv()
        both = psum[:, core, :, lanes].astype(F32) + pin[:, :, lanes].astype(F32)
        csum[:, :, lanes] = both.astype(BF16)
        for k in range(1, chips):
            chip_copy(k, q, lanes).start()

    def total(q, lanes):
        for k in range(1, chips):
            chip_copy(k, q, lanes).wait_recv()
        value = psum[chip, core, :, lanes].astype(F32) + pin[chip, :, lanes].astype(F32)
        for k in range(1, chips):
            value = value + cin[k - 1, :, lanes].astype(F32)
        return value

    gram_lanes = pl.ds(frags, rank)
    send_twin(tiles, gram_lanes, product(newt[...], newall[...], PLAIN))

    def second(q, carry):
        lanes = aligned(q, TILE)
        rest = product(newt[:, half:], counts[half:, lanes], PLAIN)
        send_twin(q, lanes, ahead_sum[:, lanes] + rest)

        @pl.when(q == 0)
        def _():
            send_chips(tiles, gram_lanes)

        @pl.when(q > 0)
        def _():
            send_chips(q - 1, aligned(q - 1, TILE))

        return carry

    lax.fori_loop(0, tiles, second, 0)
    send_chips(tiles - 1, pl.ds((tiles - 1) * TILE, TILE))

    wout[...] = newt[aligned(z, cols), :]

    for e in range(2):
        @pl.when(z != e + 1)
        def _(e=e):
            g_copies[e].wait_send()

    gram = total(tiles, gram_lanes).astype(BF16)
    gown[...] = gram.astype(F32)

    def finish(q, carry):
        lanes = aligned(q, TILE)
        denom = product(gown[...].astype(BF16), hfull[:, lanes], PLAIN)
        hout[:, lanes] = (h_ref[:, lanes].astype(F32) * total(q, lanes) / denom).astype(BF16)
        return carry

    lax.fori_loop(0, tiles, finish, 0)

    for p in range(PARTS):
        for k in range(1, chips):
            h_copy(k, p).wait_send()
        for k in range(chips):
            h_twin(k, p).wait_send()

    for e in range(2):
        @pl.when(z != e + 1)
        def _(e=e):
            w_copies[e].wait_send()

    @pl.when(inner)
    def _():
        for k in range(1, n_mol):
            g_share(k).wait_send()

    def drain(s, carry):
        @pl.when(outer)
        def _():
            edge_copy(s).wait_send()

        @pl.when(inner)
        def _():
            mid_copy(s).wait_send()
            ag_copy(s).wait_send()

        return carry

    lax.fori_loop(0, STEPS, drain, 0)

    def drain_tile(q, carry):
        lanes = aligned(q, TILE)
        twin_copy(q, lanes).wait_send()
        for k in range(1, chips):
            chip_copy(k, q, lanes).wait_send()
        return carry

    lax.fori_loop(0, tiles, drain_tile, 0)
    twin_copy(tiles, gram_lanes).wait_send()
    for k in range(1, chips):
        chip_copy(k, tiles, gram_lanes).wait_send()


def fused(n_mol, n_frag, counts, mol_factor, frag_factor):
    mols, cols = mol_factor.shape
    rows, frags = frag_factor.shape
    rank = rows * n_mol
    chips = n_mol // 2
    sub = mols // STEPS
    tiles = frags // TILE
    dma = pltpu.SemaphoreType.DMA
    vmem = pltpu.VMEM
    scratch = [
        vmem((mols, frags), BF16),
        vmem((rank, frags), BF16),
        vmem((rank, mols), BF16),
        vmem((n_frag, rows, rank), F32),
        vmem((rows, rank), F32),
        vmem((rank, rank), BF16),
        vmem((GROUP * sub, rank), F32),
        vmem((STEPS, sub, rank), BF16),
        vmem((STEPS, sub, rank), BF16),
        vmem((STEPS, sub, rank), BF16),
        vmem((STEPS, sub, rank), BF16),
        vmem((mols, rank), BF16),
        vmem((rank, mols), BF16),
        vmem((rank, frags), F32),
        vmem((chips, 2, rows, frags + rank), BF16),
        vmem((chips, rows, frags + rank), BF16),
        vmem((chips, rows, frags + rank), BF16),
        vmem((chips - 1, rows, frags + rank), BF16),
        dma,
        dma((chips - 1, PARTS)), dma((chips - 1, PARTS)),
        dma((chips, PARTS)), dma((chips, PARTS)),
        dma((2,)), dma((n_frag,)),
        dma((2,)), dma((n_frag,)),
        dma((n_mol - 1,)), dma((n_mol - 1,)),
        dma((STEPS,)), dma((STEPS,)), dma((STEPS,)), dma((STEPS,)),
        dma((STEPS,)), dma((STEPS,)),
        dma((tiles + 1,)), dma((tiles + 1,)),
        dma((chips - 1, tiles + 1)), dma((chips - 1, tiles + 1)),
    ]
    new_mol, new_frag = pl.pallas_call(
        functools.partial(kernel, n_mol, n_frag),
        out_shape=(
            jax.ShapeDtypeStruct((cols, mols), BF16),
            jax.ShapeDtypeStruct((rows, frags), BF16),
        ),
        in_specs=[
            pl.BlockSpec(memory_space=pl.ANY),
            pl.BlockSpec(memory_space=pltpu.VMEM),
            pl.BlockSpec(memory_space=pltpu.VMEM),
        ],
        out_specs=(
            pl.BlockSpec(memory_space=pltpu.VMEM),
            pl.BlockSpec(memory_space=pltpu.VMEM),
        ),
        scratch_shapes=scratch,
        compiler_params=pltpu.CompilerParams(
            collective_id=0, has_side_effects=True, vmem_limit_bytes=56 * 1024 * 1024
        ),
        cost_estimate=pl.CostEstimate(
            flops=4 * mols * frags * rank, bytes_accessed=2 * mols * frags, transcendentals=0
        ),
    )(counts, mol_factor.T, frag_factor)
    return new_mol.T, new_frag


def fits(n_mol, n_frag, mols, cols, rows, frags):
    return (
        n_mol % 2 == 0 and n_mol > 2 and n_frag == 4 and rows % 16 == 0 and cols % 16 == 0
        and mols % (STEPS * 128) == 0 and frags % (TILE * PARTS * 2) == 0
        and (rows * n_mol) % 128 == 0 and mols * frags <= 2 ** 23 and n_mol <= 8
    )


def solution(mesh):
    n_mol, n_frag = mesh.shape["mol"], mesh.shape["frag"]

    def local(counts, mol_factor, frag_factor):
        if fits(n_mol, n_frag, *mol_factor.shape, *frag_factor.shape):
            return fused(n_mol, n_frag, counts, mol_factor, frag_factor)
        return body(counts, mol_factor, frag_factor)

    return jax.shard_map(
        local,
        mesh=mesh,
        in_specs=(P("mol", "frag"), P("mol", "frag"), P("mol", "frag")),
        out_specs=(P("mol", "frag"), P("mol", "frag")),
        check_vma=False,
    )
```

```python
import functools

import jax
import jax.numpy as jnp
from jax import lax
from jax.experimental import pallas as pl
from jax.experimental.pallas import tpu as pltpu
from jax.sharding import PartitionSpec as P

CONTRACT_LAST = (((1,), (1,)), ((), ()))
CONTRACT_FIRST = (((0,), (0,)), ((), ()))


def product(left, right, dims):
    return lax.dot_general(left, right, dims, preferred_element_type=jnp.float32)


def body(counts, mol_factor, frag_factor):
    rank_cols = mol_factor.shape[1]
    rank_rows = frag_factor.shape[0]
    frag_index = lax.axis_index("frag")
    mol_index = lax.axis_index("mol")
    columns = lax.all_gather(frag_factor, "mol", axis=0, tiled=True)
    numer_whole = product(columns, counts, CONTRACT_LAST)
    gram_whole = product(columns, columns, CONTRACT_LAST)
    numer_whole, gram_whole = lax.psum((numer_whole, gram_whole), "frag")
    numer_mine = lax.dynamic_slice_in_dim(numer_whole, frag_index * rank_cols, rank_cols, 0)
    gram_mine = lax.dynamic_slice_in_dim(gram_whole, frag_index * rank_cols, rank_cols, 0)
    gram_mine = gram_mine.astype(jnp.bfloat16)
    denom_mol = product(
        lax.all_gather(mol_factor, "frag", axis=1, tiled=True), gram_mine, CONTRACT_LAST
    )
    new_mol = (mol_factor.astype(jnp.float32) * numer_mine.T / denom_mol).astype(jnp.bfloat16)
    gathered_mol = lax.all_gather(new_mol, "frag", axis=1, tiled=True)
    numer_frag = product(gathered_mol, counts, CONTRACT_FIRST)
    gram_mol = product(gathered_mol, gathered_mol, CONTRACT_FIRST)
    numer_frag, gram_mol = lax.psum((numer_frag, gram_mol), "mol")
    numer_rows = lax.dynamic_slice_in_dim(numer_frag, mol_index * rank_rows, rank_rows, 0)
    gram_rows = lax.dynamic_slice_in_dim(gram_mol, mol_index * rank_rows, rank_rows, 0)
    denom_frag = jnp.dot(
        gram_rows.astype(jnp.bfloat16), columns, preferred_element_type=jnp.float32
    )
    new_frag = (frag_factor.astype(jnp.float32) * numer_rows / denom_frag).astype(jnp.bfloat16)
    return (new_mol, new_frag)


MESH = pl.DeviceIdType.MESH
F32 = jnp.float32
BF16 = jnp.bfloat16
PLAIN = (((1,), (0,)), ((), ()))
STEPS = 16
GROUP = 2
LAG = 2
TILE = 512
PARTS = 2


def remote(src, dst, send, recv, mol, frag):
    return pltpu.make_async_remote_copy(
        src_ref=src, dst_ref=dst, send_sem=send, recv_sem=recv,
        device_id={"mol": mol, "frag": frag}, device_id_type=MESH,
    )


def aligned(index, size):
    return pl.ds(pl.multiple_of(index * size, size), size)


def kernel(
    n_mol, n_frag, counts_hbm, wt, h_ref, wout, hout,
    counts, hfull, wmine, gpart, gown, gfull, mine,
    edge_out, edge_in, mid_out, mid_in, newall, newt, ahead_sum, psum, pin, csum, cin,
    counts_sem, h_s, h_r, hc_s, hc_r, w_s, w_r, g_s, g_r, gp_s, gp_r,
    edge_s, edge_r, mid_s, mid_r, ag_s, ag_r, c1_s, c1_r, c2_s, c2_r,
):
    chips = n_mol // 2
    cols, mols = wt.shape
    rows, frags = h_ref.shape
    half = mols // 2
    sub = mols // STEPS
    rank = rows * n_mol
    block = 2 * frags // STEPS
    m = lax.axis_index("mol")
    z = lax.axis_index("frag")
    chip = m // 2
    core = m % 2
    twin = chip * 2 + 1 - core
    inner = jnp.logical_or(z == 1, z == 2)
    outer = jnp.logical_not(inner)
    pair = z + 1 - 2 * (z % 2)
    across = 3 - z
    tiles = frags // TILE
    width = frags // PARTS

    load = pltpu.make_async_copy(counts_hbm, counts, counts_sem)
    load.start()
    hfull[aligned(m, rows), :] = h_ref[...]

    @pl.when(inner)
    def _():
        wmine[aligned(z, cols), :] = wt[...]

    barrier = pltpu.get_barrier_semaphore()
    for k in range(1, n_mol):
        pl.semaphore_signal(
            barrier, inc=1, device_id={"mol": (m + k) % n_mol, "frag": z}, device_id_type=MESH)
    for k in range(1, n_frag):
        pl.semaphore_signal(
            barrier, inc=1, device_id={"mol": m, "frag": (z + k) % n_frag}, device_id_type=MESH)
    pl.semaphore_wait(barrier, n_mol - 1 + n_frag - 1)

    def h_copy(k, p):
        lanes = pl.ds(p * width, width)
        return remote(
            h_ref.at[:, lanes], hfull.at[aligned(m, rows), lanes],
            h_s.at[k - 1, p], h_r.at[k - 1, p], ((chip + k) % chips) * 2 + core, z)

    def h_twin(k, p):
        lanes = pl.ds(p * width, width)
        there = ((chip + chips - k) % chips) * 2 + core
        block = hfull.at[aligned(there, rows), lanes]
        return remote(
            h_ref.at[:, lanes] if k == 0 else block, block,
            hc_s.at[k, p], hc_r.at[k, p], twin, z)

    for p in range(PARTS):
        for k in range(1, chips):
            h_copy(k, p).start()
        h_twin(0, p).start()

    w_copies = [
        remote(wt, wmine.at[aligned(z, cols), :], w_s.at[e], w_r.at[z], m, e + 1) for e in range(2)
    ]
    for e in range(2):
        @pl.when(z != e + 1)
        def _(e=e):
            w_copies[e].start()

    for p in range(PARTS):
        for k in range(1, chips):
            h_copy(k, p).wait_recv()
            h_twin(k, p).start()
    for p in range(PARTS):
        for k in range(chips):
            h_twin(k, p).wait_recv()

    g_copies = [remote(gown, gpart.at[z], g_s.at[e], g_r.at[z], m, e + 1) for e in range(2)]
    def share_gram():
        gown[...] = product(h_ref[...], hfull[...], CONTRACT_LAST)
        for e in range(2):
            @pl.when(z != e + 1)
            def _(e=e):
                g_copies[e].start()

    load.wait()

    def g_share(k):
        block = gfull.at[aligned(m, rows), :]
        return remote(block, block, gp_s.at[k - 1], gp_r.at[k - 1], (m + k) % n_mol, z)

    def owner_ready():
        total = gown[...]
        for k in range(1, n_frag):
            there = (z + k) % n_frag
            remote(gown, gpart.at[there], g_s.at[0], g_r.at[there], m, z).wait_recv()
            total = total + gpart[there]
        gfull[aligned(m, rows), :] = total.astype(BF16)
        for k in range(1, n_mol):
            g_share(k).start()

    def owner_complete():
        for k in range(1, n_frag):
            there = (z + k) % n_frag
            remote(wt, wmine.at[aligned(there, cols), :], w_s.at[0], w_r.at[there], m, z).wait_recv()
        for k in range(1, n_mol):
            g_share(k).wait_recv()

    def edge_copy(s):
        return remote(edge_out.at[s], edge_in.at[s], edge_s.at[s], edge_r.at[s], m, pair)

    def mid_copy(s):
        return remote(mid_out.at[s], mid_in.at[s], mid_s.at[s], mid_r.at[s], m, across)

    def ag_copy(s):
        part = newall.at[aligned(s, sub), :]
        return remote(part, part, ag_s.at[s], ag_r.at[s], m, pair)

    def arrived(s):
        here = aligned(s, sub)
        newt[:, here] = newall[here, :].T

        @pl.when(s >= STEPS // 2)
        def _():
            lanes = aligned(s - STEPS // 2, block)
            ahead_sum[:, lanes] = product(newt[:, :half], counts[:half, lanes], PLAIN)

    def partial_sum(s):
        @pl.when(s % GROUP == 0)
        def _():
            rows_of = aligned(s // GROUP, GROUP * sub)
            mine[...] = product(counts[rows_of, :], hfull[...], CONTRACT_LAST)

        return mine[aligned(s % GROUP, sub), :]

    @pl.when(outer)
    def _():
        def send(s, carry):
            edge_out[s] = partial_sum(s).astype(BF16)
            edge_copy(s).start()

            @pl.when(s == GROUP - 1)
            def _():
                share_gram()

            return carry

        def take(s, carry):
            ag_copy(s).wait_recv()
            arrived(s)
            return carry

        lax.fori_loop(0, STEPS, send, 0)
        lax.fori_loop(0, STEPS, take, 0)

    @pl.when(inner)
    def _():
        def step(i, carry):
            @pl.when(i < STEPS)
            def _():
                here_sum = partial_sum(i)

                @pl.when(i == 0)
                def _():
                    share_gram()

                edge_copy(i).wait_recv()
                mid_out[i] = (here_sum + edge_in[i].astype(F32)).astype(BF16)
                mid_copy(i).start()

            @pl.when(i == LAG - 1)
            def _():
                owner_ready()

            @pl.when(i == LAG)
            def _():
                owner_complete()

            @pl.when(i >= LAG)
            def _():
                s = i - LAG
                here = aligned(s, sub)
                mid_copy(s).wait_recv()
                numer = mid_out[s].astype(F32) + mid_in[s].astype(F32)
                w = wmine[:, here].T
                denom = product(w, gfull[...], PLAIN)
                newall[here, :] = (w.astype(F32) * numer / denom).astype(BF16)
                ag_copy(s).start()
                arrived(s)

            return carry

        lax.fori_loop(0, STEPS + LAG, step, 0)

    def twin_copy(q, lanes):
        return remote(
            psum.at[:, 1 - core, :, lanes], pin.at[:, :, lanes], c1_s.at[q], c1_r.at[q], twin, z)

    def chip_copy(k, q, lanes):
        there = (chip + k) % chips
        return remote(
            csum.at[there, :, lanes], cin.at[k - 1, :, lanes],
            c2_s.at[k - 1, q], c2_r.at[k - 1, q], there * 2 + core, z)

    def send_twin(q, lanes, part):
        psum[:, :, :, lanes] = part.astype(BF16).reshape(chips, 2, rows, part.shape[1])
        twin_copy(q, lanes).start()

    def send_chips(q, lanes):
        twin_copy(q, lanes).wait_recv()
        both = psum[:, core, :, lanes].astype(F32) + pin[:, :, lanes].astype(F32)
        csum[:, :, lanes] = both.astype(BF16)
        for k in range(1, chips):
            chip_copy(k, q, lanes).start()

    def total(q, lanes):
        for k in range(1, chips):
            chip_copy(k, q, lanes).wait_recv()
        value = psum[chip, core, :, lanes].astype(F32) + pin[chip, :, lanes].astype(F32)
        for k in range(1, chips):
            value = value + cin[k - 1, :, lanes].astype(F32)
        return value

    gram_lanes = pl.ds(frags, rank)
    send_twin(tiles, gram_lanes, product(newt[...], newall[...], PLAIN))

    def second(q, carry):
        lanes = aligned(q, TILE)
        rest = product(newt[:, half:], counts[half:, lanes], PLAIN)
        send_twin(q, lanes, ahead_sum[:, lanes] + rest)

        @pl.when(q == 0)
        def _():
            send_chips(tiles, gram_lanes)

        @pl.when(q > 0)
        def _():
            send_chips(q - 1, aligned(q - 1, TILE))

        return carry

    lax.fori_loop(0, tiles, second, 0)
    send_chips(tiles - 1, pl.ds((tiles - 1) * TILE, TILE))

    wout[...] = newt[aligned(z, cols), :]

    for e in range(2):
        @pl.when(z != e + 1)
        def _(e=e):
            g_copies[e].wait_send()

    gram = total(tiles, gram_lanes).astype(BF16)
    gown[...] = gram.astype(F32)

    def finish(q, carry):
        lanes = aligned(q, TILE)
        denom = product(gown[...].astype(BF16), hfull[:, lanes], PLAIN)
        hout[:, lanes] = (h_ref[:, lanes].astype(F32) * total(q, lanes) / denom).astype(BF16)
        return carry

    lax.fori_loop(0, tiles, finish, 0)

    for p in range(PARTS):
        for k in range(1, chips):
            h_copy(k, p).wait_send()
        for k in range(chips):
            h_twin(k, p).wait_send()

    for e in range(2):
        @pl.when(z != e + 1)
        def _(e=e):
            w_copies[e].wait_send()

    @pl.when(inner)
    def _():
        for k in range(1, n_mol):
            g_share(k).wait_send()

    def drain(s, carry):
        @pl.when(outer)
        def _():
            edge_copy(s).wait_send()

        @pl.when(inner)
        def _():
            mid_copy(s).wait_send()
            ag_copy(s).wait_send()

        return carry

    lax.fori_loop(0, STEPS, drain, 0)

    def drain_tile(q, carry):
        lanes = aligned(q, TILE)
        twin_copy(q, lanes).wait_send()
        for k in range(1, chips):
            chip_copy(k, q, lanes).wait_send()
        return carry

    lax.fori_loop(0, tiles, drain_tile, 0)
    twin_copy(tiles, gram_lanes).wait_send()
    for k in range(1, chips):
        chip_copy(k, tiles, gram_lanes).wait_send()


def fused(n_mol, n_frag, counts, mol_factor, frag_factor):
    mols, cols = mol_factor.shape
    rows, frags = frag_factor.shape
    rank = rows * n_mol
    chips = n_mol // 2
    sub = mols // STEPS
    tiles = frags // TILE
    dma = pltpu.SemaphoreType.DMA
    vmem = pltpu.VMEM
    scratch = [
        vmem((mols, frags), BF16),
        vmem((rank, frags), BF16),
        vmem((rank, mols), BF16),
        vmem((n_frag, rows, rank), F32),
        vmem((rows, rank), F32),
        vmem((rank, rank), BF16),
        vmem((GROUP * sub, rank), F32),
        vmem((STEPS, sub, rank), BF16),
        vmem((STEPS, sub, rank), BF16),
        vmem((STEPS, sub, rank), BF16),
        vmem((STEPS, sub, rank), BF16),
        vmem((mols, rank), BF16),
        vmem((rank, mols), BF16),
        vmem((rank, frags), F32),
        vmem((chips, 2, rows, frags + rank), BF16),
        vmem((chips, rows, frags + rank), BF16),
        vmem((chips, rows, frags + rank), BF16),
        vmem((chips - 1, rows, frags + rank), BF16),
        dma,
        dma((chips - 1, PARTS)), dma((chips - 1, PARTS)),
        dma((chips, PARTS)), dma((chips, PARTS)),
        dma((2,)), dma((n_frag,)),
        dma((2,)), dma((n_frag,)),
        dma((n_mol - 1,)), dma((n_mol - 1,)),
        dma((STEPS,)), dma((STEPS,)), dma((STEPS,)), dma((STEPS,)),
        dma((STEPS,)), dma((STEPS,)),
        dma((tiles + 1,)), dma((tiles + 1,)),
        dma((chips - 1, tiles + 1)), dma((chips - 1, tiles + 1)),
    ]
    new_mol, new_frag = pl.pallas_call(
        functools.partial(kernel, n_mol, n_frag),
        out_shape=(
            jax.ShapeDtypeStruct((cols, mols), BF16),
            jax.ShapeDtypeStruct((rows, frags), BF16),
        ),
        in_specs=[
            pl.BlockSpec(memory_space=pl.ANY),
            pl.BlockSpec(memory_space=pltpu.VMEM),
            pl.BlockSpec(memory_space=pltpu.VMEM),
        ],
        out_specs=(
            pl.BlockSpec(memory_space=pltpu.VMEM),
            pl.BlockSpec(memory_space=pltpu.VMEM),
        ),
        scratch_shapes=scratch,
        compiler_params=pltpu.CompilerParams(
            collective_id=0, has_side_effects=True, vmem_limit_bytes=56 * 1024 * 1024
        ),
        cost_estimate=pl.CostEstimate(
            flops=4 * mols * frags * rank, bytes_accessed=2 * mols * frags, transcendentals=0
        ),
    )(counts, mol_factor.T, frag_factor)
    return new_mol.T, new_frag


def fits(n_mol, n_frag, mols, cols, rows, frags):
    return (
        n_mol % 2 == 0 and n_mol > 2 and n_frag == 4 and rows % 16 == 0 and cols % 16 == 0
        and mols % (STEPS * 128) == 0 and frags % (TILE * PARTS * 2) == 0
        and (rows * n_mol) % 128 == 0 and mols * frags <= 2 ** 23 and n_mol <= 8
    )


def solution(mesh):
    n_mol, n_frag = mesh.shape["mol"], mesh.shape["frag"]

    def local(counts, mol_factor, frag_factor):
        if fits(n_mol, n_frag, *mol_factor.shape, *frag_factor.shape):
            return fused(n_mol, n_frag, counts, mol_factor, frag_factor)
        return body(counts, mol_factor, frag_factor)

    return jax.shard_map(
        local,
        mesh=mesh,
        in_specs=(P("mol", "frag"), P("mol", "frag"), P("mol", "frag")),
        out_specs=(P("mol", "frag"), P("mol", "frag")),
        check_vma=False,
    )
```
